32 devices in a mesh: ctx: 8 (over z, y), exp: 4 (over x, core).
Axes of the slice: x: 2, y: 2, z: 4, core: 2. Of those that a mesh axis runs over, the one named last changes fastest.
Arguments:
- inputs: bfloat16 [4, 2048, 768], P('exp', 'ctx'), may hold values from -6 to 6
- norm_attn: float32 [768], replicated, may hold values from 0.5 to 1.5
- query_weight: bfloat16 [768, 768], P('exp'), may hold values from -0.21875 to 0.21875
- key_weight: bfloat16 [768, 768], P('exp'), may hold values from -0.21875 to 0.21875
- value_weight: bfloat16 [768, 768], P('exp'), may hold values from -0.21875 to 0.21875
- output_weight: bfloat16 [768, 768], P('exp'), may hold values from -6 to 6
- rel_bias: float32 [12, 32], replicated, may hold values from -4 to 4
- rel_buckets: int32 [15], replicated, may hold values from 0 to 31
- norm_ffn: float32 [768], replicated, may hold values from 0.5 to 1.5
- router: bfloat16 [768, 4], replicated, may hold values from -0.25 to 0.25
- expert_input_weight: bfloat16 [4, 3072, 768], P('exp'), may hold values from -0.21875 to 0.21875
- expert_output_weight: bfloat16 [4, 3072, 768], P('exp'), may hold values from -1.25 to 1.25
- expert_ids: int32 [4, 2048, 1], P('exp', 'ctx'), may hold values from 0 to 3; in each aligned block of 256 rows (0 to 255, 256 to 511, ..., all dimensions but the last counted through in order) at most 80 rows name the same one
- cotangent: bfloat16 [4, 2048, 768], P('exp', 'ctx'), may hold values from -6 to 6
Outputs:
- result: bfloat16 [4, 2048, 768], P('exp', 'ctx')
- grad_inputs: float32 [4, 2048, 768], P('exp', 'ctx')
- grad_norm_attn: float32 [768], replicated
- grad_w_query: float32 [768, 768], P('exp')
- grad_w_key: float32 [768, 768], P('exp')
- grad_w_value: float32 [768, 768], P('exp')
- grad_w_output: float32 [768, 768], P('exp')
- grad_rel_bias: float32 [12, 32], replicated
- grad_norm_ffn: float32 [768], replicated
- grad_router: float32 [768, 4], replicated
- grad_expert_in: float32 [4, 3072, 768], P('exp', 'ctx')
- grad_expert_out: float32 [4, 3072, 768], P('exp', 'ctx')
The draws below stay inside these ranges and needn't reach their ends.
Inputs may be any that keep to these rules, and one draw needn't show every extreme that they name: `expert_ids`: within the 256 positions of one device (aligned blocks) no expert is named more than 80 times, a bound that some block reaches.
All inputs are finite; a program needn't handle non-finite values.
Results may differ from the reference program's by a relative error of at most 0.025.
Values may be sent and summed in bfloat16 or wider, within the bound.
A program may use at most 320 MiB of HBM per device.

```python
import math
import jax
import jax.numpy as jnp
import numpy as np
from jax import lax

D = 768
HEADS = 12
HEAD_DIM = 64
FF = 3072
NBUCK = 32
TOK_DEV = 256
CAP = 80
SEQ_LEN = 2048
SEQS = 4
EXPERTS = 4
SPREAD = 15
N_CTX = 8


def with_ends(drawn, own_key, low, top_value):
    longest = drawn.shape.index(max(drawn.shape))
    spots = []
    for shift in (0, 1):
        where = [jax.random.randint(jax.random.fold_in(own_key, axis), (), 0, length) for axis, length in enumerate(drawn.shape)]
        where[longest] = (where[longest] + shift) % drawn.shape[longest]
        spots.append(tuple(where))
    return drawn.at[spots[0]].set(low).at[spots[1]].set(top_value)


def levels(rng, dims, pieces, low, largest):
    gain = 1.0
    for dim, shards_of in pieces:
        heights = jax.random.uniform(jax.random.fold_in(jax.random.fold_in(rng, 6), dim), (shards_of,), jnp.float32, low / len(pieces), largest / len(pieces))
        gain = gain * jnp.repeat(jnp.exp(heights), dims[dim] // shards_of).reshape((-1,) + (1,) * (len(dims) - 1 - dim))
    return gain


def assign_block(stream_key, own, number, rows, count, top, limit, slope):
    ranking = jax.random.permutation(stream_key, count)
    crowded, usual = load_shares(count, rows * top, limit, slope, True), load_shares(count, rows * top, limit, slope, False)
    places = jnp.arange(count)

    def named(lengths, rotation):
        used = int((lengths > 0).sum())
        fixed = max(1, used // 4)
        shifted = fixed + (places - fixed + rotation * (used - fixed)) % max(1, count - fixed)
        return jnp.zeros((count,), jnp.int32).at[ranking[jnp.where(places < fixed, places, shifted)]].set(jnp.asarray(lengths, jnp.int32))

    lengths = jnp.where(number % 4 == 0, named(crowded, number // 4), named(usual, number - number // 4 - 1))
    mixed = jax.random.permutation(jax.random.fold_in(own, 3), count)
    giver, taker = mixed[0:count // 2 * 2:2], mixed[1:count // 2 * 2:2]
    room = jnp.minimum(lengths[giver] - 1, limit - lengths[taker]) // 2
    room = jnp.where((giver == ranking[0]) | (taker == ranking[0]) | (lengths[taker] == 0), 0, jnp.maximum(room, 0))
    shifted = jax.random.randint(jax.random.fold_in(own, 4), (count // 2,), 0, 1 << 20) % (room + 1)
    lengths = lengths.at[giver].add(-shifted).at[taker].add(shifted)
    items = jnp.searchsorted(jnp.cumsum(lengths), jnp.arange(rows * top), side="right").astype(jnp.int32)
    table = items.reshape(top, rows).T
    table = table[jax.random.permutation(jax.random.fold_in(own, 1), rows)]
    rotation = jax.random.randint(jax.random.fold_in(own, 2), (rows, 1), 0, top)
    return jnp.take_along_axis(table, (jnp.arange(top)[None, :] + rotation) % top, axis=1)


def load_shares(amount, total, most, lean, full):
    loads = [(1 << 20) // math.isqrt(standing ** lean) + 1 for standing in range(1, amount + 1)]
    largest = most if full else min(most, max(-(-total // amount), total * loads[0] // sum(loads)))
    least = 1 if total - largest >= amount - 1 else 0
    holding, surplus = [largest] + [least] * (amount - 1), total - largest - least * (amount - 1)
    while surplus > 0:
        movable = [i for i in range(1, amount) if holding[i] < largest] or [i for i in range(1, amount) if holding[i] < most]
        whole, remaining = sum([loads[i] for i in movable]), surplus
        for i in movable:
            addition = min(most - holding[i], max(1, remaining * loads[i] // whole), surplus)
            holding[i] = holding[i] + addition
            surplus = surplus - addition
    return np.array(holding)


def normal_values(key, dims, scale, reach, split=(), held_as=jnp.bfloat16):
    gain = levels(key, dims, split, -0.22, 0.18) if split else 1.0
    values = jax.random.normal(key, dims, jnp.float32) * scale * gain
    return jnp.minimum(jnp.maximum(values, -reach), reach).astype(held_as)


def setup_inputs(seed: int = 0) -> dict:
    key_list = jax.random.split(jax.random.key(seed), 15)
    inputs = normal_values(key_list[0], (SEQS, SEQ_LEN, D), 1.0, 6.0, ((0, 4), (1, 8)))
    norm_attn = jnp.clip(1.0 + 0.1 * jax.random.normal(key_list[1], (D,), jnp.float32), 0.5, 1.5)
    query_weight = normal_values(key_list[2], (D, D), D ** -0.5, 0.21875, ((0, 4),))
    key_weight = normal_values(key_list[3], (D, D), D ** -0.5, 0.21875, ((0, 4),))
    value_weight = normal_values(key_list[4], (D, D), D ** -0.5, 0.21875, ((0, 4),))
    output_weight = normal_values(key_list[5], (D, D), ((SEQ_LEN / 8) ** 0.5 / D ** 0.5), 6.0, ((0, 4),))
    rel_bias = normal_values(key_list[6], (HEADS, NBUCK), 1.0, 4.0, (), jnp.float32)
    rel_buckets = with_ends(jax.random.randint(key_list[7], (SPREAD,), 0, NBUCK), jax.random.fold_in(key_list[7], 1), 0, NBUCK - 1).astype(jnp.int32)
    norm_ffn = jnp.clip(1.0 + 0.1 * jax.random.normal(key_list[8], (D,), jnp.float32), 0.5, 1.5)
    router = normal_values(key_list[9], (D, EXPERTS), (0.5 / D ** 0.5), 0.25)
    expert_input_weight = normal_values(key_list[10], (EXPERTS, FF, D), D ** -0.5, 0.21875, ((0, 4),))
    expert_output_weight = normal_values(key_list[11], (EXPERTS, FF, D), (5.0 / FF ** 0.5), 1.25, ((0, 4),))
    expert_ids_keys = jax.random.split(jax.random.fold_in(key_list[12], 1), SEQS * SEQ_LEN // TOK_DEV)
    expert_ids_turns = jax.random.permutation(jax.random.fold_in(key_list[12], 3), SEQS * SEQ_LEN // TOK_DEV)
    expert_ids = jax.vmap(lambda own, number: assign_block(jax.random.fold_in(key_list[12], 2), own, number, TOK_DEV, EXPERTS, 1, CAP, 1))(expert_ids_keys, expert_ids_turns).reshape((SEQS, SEQ_LEN, 1))
    cotangent = normal_values(key_list[13], (SEQS, SEQ_LEN, D), 1.0, 6.0, ((0, 4), (1, 8)))
    return dict(inputs=inputs, norm_attn=norm_attn, query_weight=query_weight, key_weight=key_weight, value_weight=value_weight, output_weight=output_weight, rel_bias=rel_bias, rel_buckets=rel_buckets, norm_ffn=norm_ffn, router=router, expert_input_weight=expert_input_weight, expert_output_weight=expert_output_weight, expert_ids=expert_ids, cotangent=cotangent)


EPSILON = 1e-06
PRECISE = lax.Precision.HIGHEST

@jax.custom_vjp
def reduced_precision(v):
    return lax.optimization_barrier(v.astype(jnp.bfloat16)).astype(jnp.float32)

@jax.custom_vjp
def reduced_backward(v):
    return v

def low_keep(v):
    return (reduced_precision(v), None)

def low_pass(kept, grad):
    return (grad,)

def back_keep(v):
    return (v, None)

def back_low(kept, grad):
    return (reduced_precision(grad),)
reduced_precision.defvjp(low_keep, low_pass)
reduced_backward.defvjp(back_keep, back_low)

def norm_rows(value_rows, gain_vector):
    return value_rows * lax.rsqrt(lax.optimization_barrier(jnp.mean(value_rows * value_rows, -1, keepdims=True)) + EPSILON) * gain_vector

def layer_product(form, left, right):
    return jnp.einsum(form, left, right, precision=PRECISE)

def attend(query_rows, key_rows, value_rows, offset_bias):
    length = query_rows.shape[0]
    block_rows = math.gcd(length, 512)
    key_blocks = jnp.arange(length, dtype=jnp.int32) // TOK_DEV
    score_scale = HEAD_DIM ** (-0.5)

    def one_block(packed):
        query_block, first_row = packed
        query_blocks = (first_row + jnp.arange(block_rows, dtype=jnp.int32)) // TOK_DEV
        offsets = key_blocks[None, :] - query_blocks[:, None] + N_CTX - 1
        score_bias = offset_bias[:, offsets]
        scores = reduced_backward(layer_product('qhd,khd->hqk', query_block, key_rows) * score_scale + score_bias)
        weights = jax.nn.softmax(scores, -1)
        return layer_product('hqk,khd->qhd', reduced_precision(weights), value_rows)
    blocks = query_rows.reshape(length // block_rows, block_rows, HEADS, HEAD_DIM)
    firsts = jnp.arange(length // block_rows, dtype=jnp.int32) * block_rows
    attention_mixed = lax.map(jax.checkpoint(one_block), (blocks, firsts))
    return attention_mixed.reshape(length, HEADS * HEAD_DIM)

def layer(inputs, norm_attn, query_weight, key_weight, value_weight, output_weight, rel_bias, norm_ffn, router, expert_input_weight, expert_output_weight, rel_buckets, expert_ids):
    first_normed = reduced_precision(norm_rows(inputs, norm_attn))
    query_rows = reduced_backward(reduced_precision(layer_product('yca,ap->ycp', first_normed, query_weight)))
    key_rows = reduced_backward(reduced_precision(layer_product('yca,ap->ycp', first_normed, key_weight)))
    value_rows = reduced_backward(reduced_precision(layer_product('yca,ap->ycp', first_normed, value_weight)))
    offset_bias = rel_bias[:, rel_buckets]
    head_shape = (SEQS, SEQ_LEN, HEADS, HEAD_DIM)

    def attend_sequence(packed):
        return attend(packed[0], packed[1], packed[2], offset_bias)
    attention_mixed = lax.map(attend_sequence, (query_rows.reshape(head_shape), key_rows.reshape(head_shape), value_rows.reshape(head_shape)))
    attention_mixed = reduced_backward(reduced_precision(attention_mixed))
    first_residual = inputs + reduced_backward(layer_product('yca,ap->ycp', attention_mixed, output_weight))
    second_normed = reduced_precision(norm_rows(first_residual, norm_ffn))
    router_logits = layer_product('yca,ap->ycp', second_normed, router)
    probs = jax.nn.softmax(router_logits, -1)
    chosen = (expert_ids[..., 0][..., None] == jnp.arange(EXPERTS, dtype=jnp.int32)).astype(jnp.float32)
    gate = lax.optimization_barrier(jnp.sum(probs * chosen, -1, keepdims=True))
    dispatched_rows = reduced_backward(second_normed)
    picked = jnp.zeros_like(inputs)
    for chosen_expert_index in range(EXPERTS):
        hidden_preactivation = reduced_backward(layer_product('prk,jk->prj', dispatched_rows, expert_input_weight[chosen_expert_index]))
        hidden_activation = reduced_precision(jax.nn.gelu(hidden_preactivation, approximate=False))
        expert_result = reduced_backward(reduced_precision(layer_product('jxm,me->jxe', hidden_activation, expert_output_weight[chosen_expert_index])))
        picked = picked + chosen[..., chosen_expert_index:chosen_expert_index + 1] * expert_result
    return first_residual + gate * picked

def reference(inputs, norm_attn, query_weight, key_weight, value_weight, output_weight, rel_bias, rel_buckets, norm_ffn, router, expert_input_weight, expert_output_weight, expert_ids, cotangent):
    floats = (inputs.astype(jnp.float32), norm_attn, query_weight.astype(jnp.float32), key_weight.astype(jnp.float32), value_weight.astype(jnp.float32), output_weight.astype(jnp.float32), rel_bias, norm_ffn, router.astype(jnp.float32), expert_input_weight.astype(jnp.float32), expert_output_weight.astype(jnp.float32))

    def bound_layer(*arrays):
        return layer(*arrays, rel_buckets, expert_ids)
    result, pull = jax.vjp(bound_layer, *floats)
    grads = pull(cotangent.astype(jnp.float32))
    return (result.astype(jnp.bfloat16), grads[0], grads[1], grads[2], grads[3], grads[4], grads[5], grads[6], grads[7], grads[8], grads[9], grads[10])
```

```python
import functools
import math

import jax
import jax.numpy as jnp
from jax import lax
from jax.experimental import pallas as pl
from jax.experimental.pallas import tpu as pltpu
from jax.sharding import PartitionSpec as P

EPSILON = 1e-06
PRECISE = lax.Precision.HIGHEST
VERY_LOW = -1e30
LONGEST_RING = 16
F32 = jnp.float32
LOW = jnp.bfloat16


def norm_rows(value_rows, gain_vector):
    return (
        value_rows
        * lax.rsqrt(jnp.mean(value_rows * value_rows, -1, keepdims=True) + EPSILON)
        * gain_vector
    )


def one_hot(indices, class_count):
    return (indices[:, None] == jnp.arange(class_count, dtype=jnp.int32)[None, :]).astype(F32)


def gelu_exact(value_rows):
    return jax.nn.gelu(value_rows, approximate=False)


def dot_f32(left, right, left_dim, right_dim):
    return lax.dot_general(
        left, right, (((left_dim,), (right_dim,)), ((), ())), preferred_element_type=F32
    )


class Ring:
    def __init__(self):
        self.size = size = lax.axis_size("ctx")
        order = list(range(0, size, 2)) + list(range(size - 1, 0, -2))
        self.order = jnp.array(order, jnp.int32)
        self.place = jnp.array([order.index(i) for i in range(size)], jnp.int32)[
            lax.axis_index("ctx")
        ]
        self.up = [(order[i], order[(i + 1) % size]) for i in range(size)]
        self.down = [(there, here) for here, there in self.up]

    def owner(self, step):
        return self.order[(self.place + step + 2 * self.size) % self.size]

    def gather(self, block):
        size = self.size
        if size > LONGEST_RING:
            return lax.all_gather(block, "ctx", axis=0)
        rows = block.shape[0]
        whole = jnp.zeros((size,) + block.shape, block.dtype)
        whole = lax.dynamic_update_slice(whole, block[None], (self.owner(0), 0, 0))
        rising = falling = block
        for step in range(1, size // 2):
            rising = lax.ppermute(rising, "ctx", self.up)
            falling = lax.ppermute(falling, "ctx", self.down)
            whole = lax.dynamic_update_slice(whole, rising[None], (self.owner(-step), 0, 0))
            whole = lax.dynamic_update_slice(whole, falling[None], (self.owner(step), 0, 0))
        half = rows // 2
        far = self.owner(size // 2)
        rising = lax.ppermute(rising[:half], "ctx", self.up)
        falling = lax.ppermute(falling[half:], "ctx", self.down)
        whole = lax.dynamic_update_slice(whole, rising[None], (far, 0, 0))
        whole = lax.dynamic_update_slice(whole, falling[None], (far, half, 0))
        return whole

    def scatter(self, pieces):
        if self.size > LONGEST_RING:
            return [
                lax.psum_scatter(piece, "ctx", scatter_dimension=0).astype(F32) for piece in pieces
            ]
        signs = [1 if i % 2 else -1 for i in range(len(pieces))]
        ways = [self.down if i % 2 else self.up for i in range(len(pieces))]

        def own(i, step):
            return lax.dynamic_index_in_dim(
                pieces[i], self.owner(signs[i] * step), 0, keepdims=False
            )

        sums = [own(i, 1) for i in range(len(pieces))]
        for step in range(2, self.size + 1):
            for i in range(len(pieces)):
                arrived = lax.ppermute(sums[i], "ctx", ways[i])
                term = own(i, step if step < self.size else 0)
                total = arrived.astype(F32) + term.astype(F32)
                sums[i] = total if step == self.size else total.astype(pieces[i].dtype)
        return sums


def flips(bit):
    return [(i, i ^ bit) for i in range(lax.axis_size("exp"))]


def exp_gather(shard):
    count = lax.axis_size("exp")
    me = lax.axis_index("exp")
    held = {0: shard}
    bit = count // 2
    while bit:
        for key in list(held):
            held[key | bit] = lax.ppermute(held[key], "exp", flips(bit))
        bit //= 2
    stacked = jnp.stack([held[k] for k in range(count)])
    return stacked[me ^ jnp.arange(count)]


def exp_scatter(parts):
    count = lax.axis_size("exp")
    me = lax.axis_index("exp")
    held = {
        k: lax.dynamic_index_in_dim(parts, me ^ k, 0, keepdims=False) for k in range(count)
    }
    bit = 1
    while bit < count:
        for key in [k for k in held if k & bit]:
            arrived = lax.ppermute(held.pop(key), "exp", flips(bit))
            total = held[key ^ bit].astype(F32) + arrived.astype(F32)
            held[key ^ bit] = total.astype(parts.dtype)
        bit *= 2
    return held[0]


def own_head(rows, head, width):
    lanes = lax.broadcasted_iota(jnp.int32, rows.shape, 1) // width
    return jnp.where(lanes == head, rows, jnp.zeros_like(rows))


def attend_kernel(
    width, block, bias_ref, q_ref, k_ref, v_ref, out_ref, lse_ref, score_ref, top_ref, sum_ref, acc_ref
):
    chunk = pl.program_id(1)
    blocks = k_ref.shape[0] // block
    heads = q_ref.shape[1] // width

    @pl.when(chunk == 0)
    def _():
        top_ref[...] = jnp.full_like(top_ref, VERY_LOW)
        sum_ref[...] = jnp.zeros_like(sum_ref)
        acc_ref[...] = jnp.zeros_like(acc_ref)

    for head in range(heads):
        query = own_head(q_ref[...], head, width)
        old_top = top_ref[head : head + 1, :]
        top = old_top
        for b in range(blocks):
            score = dot_f32(k_ref[b * block : (b + 1) * block, :], query, 1, 1)
            score = score + bias_ref[pl.program_id(0) * heads + head, chunk * blocks + b]
            score_ref[b * block : (b + 1) * block, :] = score
            top = jnp.maximum(top, jnp.max(score, 0, keepdims=True))
        rescale = jnp.exp(old_top - top)
        total = sum_ref[head : head + 1, :] * rescale
        acc = acc_ref[head] * rescale
        for b in range(blocks):
            weight = jnp.exp(score_ref[b * block : (b + 1) * block, :] - top)
            total = total + jnp.sum(weight, 0, keepdims=True)
            acc = acc + dot_f32(v_ref[b * block : (b + 1) * block, :], weight.astype(LOW), 0, 0)
        top_ref[head : head + 1, :] = top
        sum_ref[head : head + 1, :] = total
        acc_ref[head] = acc

    @pl.when(chunk == pl.num_programs(1) - 1)
    def _():
        parts = []
        for head in range(heads):
            total = sum_ref[head : head + 1, :]
            parts.append(acc_ref[head, head * width : (head + 1) * width, :] / total)
            lse_ref[0, head : head + 1, :] = top_ref[head : head + 1, :] + jnp.log(total)
        out_ref[...] = jnp.concatenate(parts, 0).T


def pull_kernel(
    width, block, scale, bias_ref, q_ref, g_ref, o_ref, lse_ref, k_ref, v_ref,
    dq_ref, dk_ref, dv_ref, table_ref, acc_ref,
):
    chunk = pl.program_id(1)
    blocks = k_ref.shape[0] // block
    heads = q_ref.shape[1] // width

    @pl.when(chunk == 0)
    def _():
        acc_ref[...] = jnp.zeros_like(acc_ref)

    products = (g_ref[...].astype(F32) * o_ref[...]).T
    ones = jnp.ones((8, block), LOW)
    queries = [own_head(q_ref[...], head, width) for head in range(heads)]
    grads = [own_head(g_ref[...], head, width) for head in range(heads)]
    deltas = [
        jnp.sum(products[head * width : (head + 1) * width, :], 0, keepdims=True)
        for head in range(heads)
    ]
    for b in range(blocks):
        rows = slice(b * block, (b + 1) * block)
        keys, values = k_ref[rows, :], v_ref[rows, :]
        grad_key = grad_value = None
        for head in range(heads):
            shift = lse_ref[0, head : head + 1, :] - (
                bias_ref[pl.program_id(0) * heads + head, chunk * blocks + b]
            )
            weight = jnp.exp(dot_f32(keys, queries[head], 1, 1) - shift)
            slope = dot_f32(values, grads[head], 1, 1)
            score = (weight * (slope - deltas[head])).astype(LOW)
            more_key = dot_f32(score, queries[head], 1, 0)
            more_value = dot_f32(weight.astype(LOW), grads[head], 1, 0)
            grad_key = more_key if head == 0 else grad_key + more_key
            grad_value = more_value if head == 0 else grad_value + more_value
            acc_ref[head] += dot_f32(keys, score, 0, 0)
            table_ref[0, head, b : b + 1, :] = dot_f32(ones, score, 1, 0)[:1]
        dk_ref[rows, :] = grad_key.astype(LOW)
        dv_ref[rows, :] = grad_value.astype(LOW)

    @pl.when(chunk == pl.num_programs(1) - 1)
    def _():
        parts = [acc_ref[head, head * width : (head + 1) * width, :] for head in range(heads)]
        dq_ref[...] = (jnp.concatenate(parts, 0).T * scale).astype(LOW)


def attention_calls(rows, length, model_width, head_count, head_width):
    lanes = max(128, head_width)
    heads = lanes // head_width
    pairs = head_count // heads
    block = rows
    chunk = block * math.gcd(length // block, 8)
    chunks = length // chunk
    table_blocks = length // block
    local = pl.BlockSpec((rows, lanes), lambda p, c: (0, p))
    remote_keys = pl.BlockSpec((chunk, lanes), lambda p, c: (c, p))
    remote_values = pl.BlockSpec((chunk, lanes), lambda p, c: (c, p + pairs))
    bias_spec = pl.BlockSpec(memory_space=pltpu.SMEM)
    stats = pl.BlockSpec((1, heads, rows), lambda p, c: (p, 0, 0))
    params = pltpu.CompilerParams(
        dimension_semantics=("arbitrary", "arbitrary"), vmem_limit_bytes=40 * 1024 * 1024
    )
    flops = 2 * rows * length * lanes * head_count
    attend = pl.pallas_call(
        functools.partial(attend_kernel, head_width, block),
        grid=(pairs, chunks),
        in_specs=[bias_spec, local, remote_keys, remote_values],
        out_specs=[local, stats],
        out_shape=[
            jax.ShapeDtypeStruct((rows, model_width), F32),
            jax.ShapeDtypeStruct((pairs, heads, rows), F32),
        ],
        scratch_shapes=[
            pltpu.VMEM((chunk, rows), F32),
            pltpu.VMEM((heads, rows), F32),
            pltpu.VMEM((heads, rows), F32),
            pltpu.VMEM((heads, lanes, rows), F32),
        ],
        compiler_params=params,
        cost_estimate=pl.CostEstimate(
            flops=4 * flops,
            bytes_accessed=4 * length * model_width,
            transcendentals=rows * length * head_count,
        ),
    )
    pull = pl.pallas_call(
        functools.partial(pull_kernel, head_width, block, head_width ** (-0.5)),
        grid=(pairs, chunks),
        in_specs=[bias_spec, local, local, local, stats, remote_keys, remote_values],
        out_specs=[
            local,
            remote_keys,
            remote_keys,
            pl.BlockSpec((1, heads, chunk // block, rows), lambda p, c: (p, 0, c, 0)),
        ],
        out_shape=[
            jax.ShapeDtypeStruct((rows, model_width), LOW),
            jax.ShapeDtypeStruct((length, model_width), LOW),
            jax.ShapeDtypeStruct((length, model_width), LOW),
            jax.ShapeDtypeStruct((pairs, heads, table_blocks, rows), F32),
        ],
        scratch_shapes=[pltpu.VMEM((heads, lanes, rows), F32)],
        compiler_params=params,
        cost_estimate=pl.CostEstimate(
            flops=10 * flops,
            bytes_accessed=8 * length * model_width,
            transcendentals=rows * length * head_count,
        ),
    )
    return attend, pull


def to_experts(rows, expert_count, capacity):
    return lax.all_to_all(
        rows.reshape(expert_count, capacity, rows.shape[-1]),
        "exp",
        split_axis=0,
        concat_axis=0,
        tiled=True,
    ).reshape(-1, rows.shape[-1])


def per_device(
    inputs,
    norm_attn,
    query_weight,
    key_weight,
    value_weight,
    output_weight,
    rel_bias,
    rel_buckets,
    norm_ffn,
    router,
    expert_input_weight,
    expert_output_weight,
    expert_ids,
    cotangent,
):
    rows = inputs.shape[1]
    width = inputs.shape[2]
    head_count = rel_bias.shape[0]
    head_width = width // head_count
    offset_count = rel_buckets.shape[0]
    expert_count = router.shape[1]
    shards = lax.axis_size("exp")
    cycle_size = lax.axis_size("ctx")
    cycle_index = lax.axis_index("ctx")
    length = rows * cycle_size
    capacity = rows * 5 // (4 * shards)
    score_scale = head_width ** (-0.5)
    ring = Ring()
    attend, pull = attention_calls(rows, length, width, head_count, head_width)

    input_rows = inputs[0].astype(F32)
    first_normed = norm_rows(input_rows, norm_attn).astype(LOW)
    all_normed = ring.gather(first_normed)
    own_weights = jnp.concatenate([key_weight, value_weight, query_weight, output_weight], 1)
    full_weights = exp_gather(own_weights).reshape(width, 4 * width)
    key_value_weight = full_weights[:, : 2 * width]
    full_query = full_weights[:, 2 * width : 3 * width]
    full_output = full_weights[:, 3 * width :]

    normed_all = all_normed.reshape(length, width)
    key_value = dot_f32(normed_all, key_value_weight, 1, 0).astype(LOW)
    query_low = dot_f32(first_normed, full_query, 1, 0).astype(LOW)
    query_scaled = (query_low.astype(F32) * score_scale).astype(LOW)

    picker = one_hot(rel_buckets, rel_bias.shape[1])
    offset_bias = jnp.dot(rel_bias, picker.T, precision=PRECISE)
    offset_hot = one_hot(
        jnp.arange(cycle_size, dtype=jnp.int32) - cycle_index + cycle_size - 1, offset_count
    )
    block_bias = jnp.dot(offset_bias, offset_hot.T, precision=PRECISE)

    attended, log_total = attend(block_bias, query_scaled, key_value, key_value)
    attended_low = attended.astype(LOW)
    first_residual = input_rows + dot_f32(attended_low, full_output, 1, 0)
    second_normed = norm_rows(first_residual, norm_ffn).astype(LOW)
    router_logits = jnp.dot(second_normed, router, preferred_element_type=F32)
    probs = jax.nn.softmax(router_logits, -1)
    expert_rows = expert_ids[0, :, 0]
    chosen = one_hot(expert_rows, expert_count)
    gate = jnp.sum(probs * chosen, -1)
    slot_rank = jnp.sum((jnp.cumsum(chosen, 0) - 1.0) * chosen, -1).astype(jnp.int32)
    targets = expert_rows * capacity + slot_rank
    dispatch = one_hot(targets, expert_count * capacity).astype(LOW)
    grad_result = cotangent[0].astype(F32)
    grad_made = (gate[:, None] * grad_result).astype(LOW)

    outgoing = jnp.concatenate([second_normed, grad_made], 1)
    send_rows = dot_f32(dispatch, outgoing, 0, 0).astype(LOW)
    arrived = to_experts(send_rows, expert_count, capacity)
    expert_rows_in = arrived[:, :width]
    grad_rows = arrived[:, width:]
    weight_in = expert_input_weight[0]
    weight_out = expert_output_weight[0]
    hidden_preactivation = dot_f32(expert_rows_in, weight_in, 1, 1)
    hidden, gelu_pull = jax.vjp(gelu_exact, hidden_preactivation)
    hidden_low = hidden.astype(LOW)
    grad_hidden = dot_f32(grad_rows, weight_out, 1, 1)
    grad_pre = gelu_pull(grad_hidden)[0].astype(LOW)
    made_low = dot_f32(hidden_low, weight_out, 1, 0).astype(LOW)
    grad_sent = dot_f32(grad_pre, weight_in, 1, 0).astype(LOW)
    returned = to_experts(jnp.concatenate([made_low, grad_sent], 1), expert_count, capacity)
    back = dot_f32(dispatch, returned, 1, 0)
    picked = back[:, :width]
    grad_from_expert = back[:, width:]

    unit_rows = weight_in.shape[0] // cycle_size
    in_weight_part = dot_f32(grad_pre, expert_rows_in, 0, 0).astype(LOW)
    out_weight_part = dot_f32(hidden_low, grad_rows, 0, 0).astype(LOW)
    expert_pieces = [
        in_weight_part.reshape(cycle_size, unit_rows, width),
        out_weight_part.reshape(cycle_size, unit_rows, width),
    ]
    expert_in_grad, expert_out_grad = ring.scatter(expert_pieces)

    result = (first_residual + gate[:, None] * picked).astype(LOW)
    grad_gate = jnp.sum(grad_result * picked, -1)
    grad_probs = chosen * grad_gate[:, None]
    grad_logits = probs * (grad_probs - jnp.sum(probs * grad_probs, -1, keepdims=True))
    router_part = jnp.dot(second_normed.astype(F32).T, grad_logits, precision=PRECISE)
    grad_two = grad_from_expert + jnp.dot(grad_logits, router.astype(F32).T, precision=PRECISE)
    norm_pull_two = jax.vjp(norm_rows, first_residual, norm_ffn)[1]
    grad_resid_part, ffn_gain_part = norm_pull_two(grad_two)
    grad_residual = grad_result + grad_resid_part
    grad_branch = grad_residual.astype(LOW)
    output_part = dot_f32(attended_low, grad_branch, 0, 0).astype(LOW)
    grad_attended = dot_f32(grad_branch, full_output, 1, 1).astype(LOW)

    grad_query_low, grad_key_part, grad_value_part, table_rows = pull(
        block_bias, query_scaled, grad_attended, attended, log_total, key_value, key_value
    )
    grad_normed_part = (
        dot_f32(grad_key_part, key_value_weight[:, :width], 1, 1)
        + dot_f32(grad_value_part, key_value_weight[:, width:], 1, 1)
    ).astype(LOW)
    normed_blocks = grad_normed_part.reshape(cycle_size, rows, width)
    half = rows // 2
    normed_sums = ring.scatter([normed_blocks[:, :half], normed_blocks[:, half:]])
    query_part = dot_f32(first_normed, grad_query_low, 0, 0).astype(LOW)
    key_part = dot_f32(normed_all, grad_key_part, 0, 0).astype(LOW)
    value_part = dot_f32(normed_all, grad_value_part, 0, 0).astype(LOW)
    dense_parts = jnp.concatenate([query_part, key_part, value_part, output_part], 1)
    dense_shard = exp_scatter(dense_parts.reshape(shards, width // shards, 4 * width))

    grad_normed = jnp.concatenate(normed_sums, 0) + dot_f32(grad_query_low, full_query, 1, 1)
    norm_pull_one = jax.vjp(norm_rows, input_rows, norm_attn)[1]
    grad_input_part, attn_gain_part = norm_pull_one(grad_normed)
    grad_inputs = grad_residual + grad_input_part

    dense_total = reduce_dense(ring, dense_shard)
    query_total, key_total, value_total, output_total = jnp.split(dense_total, 4, 1)

    grad_table = jnp.sum(table_rows.reshape(head_count, cycle_size, rows), -1)
    bias_part = jnp.dot(jnp.dot(grad_table, offset_hot, precision=PRECISE), picker, precision=PRECISE)
    small = [attn_gain_part, ffn_gain_part, router_part, bias_part]
    flat = jnp.concatenate([part.reshape(-1) for part in small])
    flat = lax.psum(flat, ("ctx", "exp"))
    totals, start = [], 0
    for part in small:
        totals.append(flat[start : start + part.size].reshape(part.shape))
        start += part.size
    attn_gain_total, ffn_gain_total, router_total, bias_total = totals
    return (
        result[None],
        grad_inputs[None],
        attn_gain_total,
        query_total,
        key_total,
        value_total,
        output_total,
        bias_total,
        ffn_gain_total,
        router_total,
        expert_in_grad[None],
        expert_out_grad[None],
    )


def reduce_dense(ring, shard):
    size = ring.size
    flat = shard.reshape(size, -1, 128)
    half = flat.shape[1] // 2
    sums = ring.scatter([flat[:, :half], flat[:, half:]])
    mine = jnp.concatenate(sums, 0).astype(LOW)
    return ring.gather(mine).reshape(shard.shape).astype(F32)


def solution(mesh):
    return jax.shard_map(
        per_device,
        mesh=mesh,
        in_specs=(
            P("exp", "ctx", None),
            P(),
            P("exp", None),
            P("exp", None),
            P("exp", None),
            P("exp", None),
            P(),
            P(),
            P(),
            P(),
            P("exp", None, None),
            P("exp", None, None),
            P("exp", "ctx", None),
            P("exp", "ctx", None),
        ),
        out_specs=(
            P("exp", "ctx", None),
            P("exp", "ctx", None),
            P(),
            P("exp", None),
            P("exp", None),
            P("exp", None),
            P("exp", None),
            P(),
            P(),
            P(),
            P("exp", "ctx", None),
            P("exp", "ctx", None),
        ),
        check_vma=False,
    )
```

```python
import functools
import math

import jax
import jax.numpy as jnp
from jax import lax
from jax.experimental import pallas as pl
from jax.experimental.pallas import tpu as pltpu
from jax.sharding import PartitionSpec as P

EPSILON = 1e-06
PRECISE = lax.Precision.HIGHEST
VERY_LOW = -1e30
LONGEST_RING = 16
F32 = jnp.float32
LOW = jnp.bfloat16


def norm_rows(value_rows, gain_vector):
    return (
        value_rows
        * lax.rsqrt(jnp.mean(value_rows * value_rows, -1, keepdims=True) + EPSILON)
        * gain_vector
    )


def one_hot(indices, class_count):
    return (indices[:, None] == jnp.arange(class_count, dtype=jnp.int32)[None, :]).astype(F32)


def gelu_exact(value_rows):
    return jax.nn.gelu(value_rows, approximate=False)


def dot_f32(left, right, left_dim, right_dim):
    return lax.dot_general(
        left, right, (((left_dim,), (right_dim,)), ((), ())), preferred_element_type=F32
    )


class Ring:
    def __init__(self):
        self.size = size = lax.axis_size("ctx")
        order = list(range(0, size, 2)) + list(range(size - 1, 0, -2))
        self.order = jnp.array(order, jnp.int32)
        self.place = jnp.array([order.index(i) for i in range(size)], jnp.int32)[
            lax.axis_index("ctx")
        ]
        self.up = [(order[i], order[(i + 1) % size]) for i in range(size)]
        self.down = [(there, here) for here, there in self.up]

    def owner(self, step):
        return self.order[(self.place + step + 2 * self.size) % self.size]

    def gather(self, block):
        size = self.size
        if size > LONGEST_RING:
            return lax.all_gather(block, "ctx", axis=0)
        rows = block.shape[0]
        whole = jnp.zeros((size,) + block.shape, block.dtype)
        whole = lax.dynamic_update_slice(whole, block[None], (self.owner(0), 0, 0))
        rising = falling = block
        for step in range(1, size // 2):
            rising = lax.ppermute(rising, "ctx", self.up)
            falling = lax.ppermute(falling, "ctx", self.down)
            whole = lax.dynamic_update_slice(whole, rising[None], (self.owner(-step), 0, 0))
            whole = lax.dynamic_update_slice(whole, falling[None], (self.owner(step), 0, 0))
        half = rows // 2
        far = self.owner(size // 2)
        rising = lax.ppermute(rising[:half], "ctx", self.up)
        falling = lax.ppermute(falling[half:], "ctx", self.down)
        whole = lax.dynamic_update_slice(whole, rising[None], (far, 0, 0))
        whole = lax.dynamic_update_slice(whole, falling[None], (far, half, 0))
        return whole

    def scatter(self, pieces):
        if self.size > LONGEST_RING:
            return [
                lax.psum_scatter(piece, "ctx", scatter_dimension=0).astype(F32) for piece in pieces
            ]
        signs = [1 if i % 2 else -1 for i in range(len(pieces))]
        ways = [self.down if i % 2 else self.up for i in range(len(pieces))]

        def own(i, step):
            return lax.dynamic_index_in_dim(
                pieces[i], self.owner(signs[i] * step), 0, keepdims=False
            )

        sums = [own(i, 1) for i in range(len(pieces))]
        for step in range(2, self.size + 1):
            for i in range(len(pieces)):
                arrived = lax.ppermute(sums[i], "ctx", ways[i])
                term = own(i, step if step < self.size else 0)
                total = arrived.astype(F32) + term.astype(F32)
                sums[i] = total if step == self.size else total.astype(pieces[i].dtype)
        return sums


def flips(bit):
    return [(i, i ^ bit) for i in range(lax.axis_size("exp"))]


def exp_gather(shard):
    count = lax.axis_size("exp")
    me = lax.axis_index("exp")
    held = {0: shard}
    bit = count // 2
    while bit:
        for key in list(held):
            held[key | bit] = lax.ppermute(held[key], "exp", flips(bit))
        bit //= 2
    stacked = jnp.stack([held[k] for k in range(count)])
    return stacked[me ^ jnp.arange(count)]


def exp_scatter(parts):
    count = lax.axis_size("exp")
    me = lax.axis_index("exp")
    held = {
        k: lax.dynamic_index_in_dim(parts, me ^ k, 0, keepdims=False) for k in range(count)
    }
    bit = 1
    while bit < count:
        for key in [k for k in held if k & bit]:
            arrived = lax.ppermute(held.pop(key), "exp", flips(bit))
            total = held[key ^ bit].astype(F32) + arrived.astype(F32)
            held[key ^ bit] = total.astype(parts.dtype)
        bit *= 2
    return held[0]


def butterfly_sum(term):
    for axis in ("exp", "ctx"):
        count = lax.axis_size(axis)
        if count & (count - 1):
            term = lax.psum(term, axis)
            continue
        bit = 1
        while bit < count:
            pairs = [(i, i ^ bit) for i in range(count)]
            term = term + lax.ppermute(term, axis, pairs)
            bit *= 2
    return term


def own_head(rows, head, width):
    lanes = lax.broadcasted_iota(jnp.int32, rows.shape, 1) // width
    return jnp.where(lanes == head, rows, jnp.zeros_like(rows))


def attend_kernel(
    width, block, bias_ref, q_ref, k_ref, v_ref, out_ref, lse_ref, score_ref, top_ref, sum_ref, acc_ref
):
    chunk = pl.program_id(1)
    blocks = k_ref.shape[0] // block
    heads = q_ref.shape[1] // width

    @pl.when(chunk == 0)
    def _():
        top_ref[...] = jnp.full_like(top_ref, VERY_LOW)
        sum_ref[...] = jnp.zeros_like(sum_ref)
        acc_ref[...] = jnp.zeros_like(acc_ref)

    for head in range(heads):
        query = own_head(q_ref[...], head, width)
        old_top = top_ref[head : head + 1, :]
        top = old_top
        for b in range(blocks):
            score = dot_f32(k_ref[b * block : (b + 1) * block, :], query, 1, 1)
            score = score + bias_ref[pl.program_id(0) * heads + head, chunk * blocks + b]
            score_ref[b * block : (b + 1) * block, :] = score
            top = jnp.maximum(top, jnp.max(score, 0, keepdims=True))
        rescale = jnp.exp(old_top - top)
        total = sum_ref[head : head + 1, :] * rescale
        acc = acc_ref[head] * rescale
        for b in range(blocks):
            weight = jnp.exp(score_ref[b * block : (b + 1) * block, :] - top)
            total = total + jnp.sum(weight, 0, keepdims=True)
            acc = acc + dot_f32(v_ref[b * block : (b + 1) * block, :], weight.astype(LOW), 0, 0)
        top_ref[head : head + 1, :] = top
        sum_ref[head : head + 1, :] = total
        acc_ref[head] = acc

    @pl.when(chunk == pl.num_programs(1) - 1)
    def _():
        parts = []
        for head in range(heads):
            total = sum_ref[head : head + 1, :]
            parts.append(acc_ref[head, head * width : (head + 1) * width, :] / total)
            lse_ref[0, head : head + 1, :] = top_ref[head : head + 1, :] + jnp.log(total)
        out_ref[...] = jnp.concatenate(parts, 0).T


def pull_kernel(
    width, block, scale, bias_ref, q_ref, g_ref, o_ref, lse_ref, k_ref, v_ref,
    dq_ref, dk_ref, dv_ref, table_ref, acc_ref,
):
    chunk = pl.program_id(1)
    blocks = k_ref.shape[0] // block
    heads = q_ref.shape[1] // width

    @pl.when(chunk == 0)
    def _():
        acc_ref[...] = jnp.zeros_like(acc_ref)

    products = (g_ref[...].astype(F32) * o_ref[...]).T
    ones = jnp.ones((8, block), LOW)
    queries = [own_head(q_ref[...], head, width) for head in range(heads)]
    grads = [own_head(g_ref[...], head, width) for head in range(heads)]
    deltas = [
        jnp.sum(products[head * width : (head + 1) * width, :], 0, keepdims=True)
        for head in range(heads)
    ]
    for b in range(blocks):
        rows = slice(b * block, (b + 1) * block)
        keys, values = k_ref[rows, :], v_ref[rows, :]
        grad_key = grad_value = None
        for head in range(heads):
            shift = lse_ref[0, head : head + 1, :] - (
                bias_ref[pl.program_id(0) * heads + head, chunk * blocks + b]
            )
            weight = jnp.exp(dot_f32(keys, queries[head], 1, 1) - shift)
            slope = dot_f32(values, grads[head], 1, 1)
            score = (weight * (slope - deltas[head])).astype(LOW)
            more_key = dot_f32(score, queries[head], 1, 0)
            more_value = dot_f32(weight.astype(LOW), grads[head], 1, 0)
            grad_key = more_key if head == 0 else grad_key + more_key
            grad_value = more_value if head == 0 else grad_value + more_value
            acc_ref[head] += dot_f32(keys, score, 0, 0)
            table_ref[0, head, b : b + 1, :] = dot_f32(ones, score, 1, 0)[:1]
        dk_ref[rows, :] = grad_key.astype(LOW)
        dv_ref[rows, :] = grad_value.astype(LOW)

    @pl.when(chunk == pl.num_programs(1) - 1)
    def _():
        parts = [acc_ref[head, head * width : (head + 1) * width, :] for head in range(heads)]
        dq_ref[...] = (jnp.concatenate(parts, 0).T * scale).astype(LOW)


def attention_calls(rows, length, model_width, head_count, head_width):
    lanes = max(128, head_width)
    heads = lanes // head_width
    pairs = head_count // heads
    block = rows
    chunk = block * math.gcd(length // block, 8)
    chunks = length // chunk
    table_blocks = length // block
    local = pl.BlockSpec((rows, lanes), lambda p, c: (0, p))
    remote_keys = pl.BlockSpec((chunk, lanes), lambda p, c: (c, p))
    remote_values = pl.BlockSpec((chunk, lanes), lambda p, c: (c, p + pairs))
    bias_spec = pl.BlockSpec(memory_space=pltpu.SMEM)
    stats = pl.BlockSpec((1, heads, rows), lambda p, c: (p, 0, 0))
    params = pltpu.CompilerParams(
        dimension_semantics=("arbitrary", "arbitrary"), vmem_limit_bytes=40 * 1024 * 1024
    )
    flops = 2 * rows * length * lanes * head_count
    attend = pl.pallas_call(
        functools.partial(attend_kernel, head_width, block),
        grid=(pairs, chunks),
        in_specs=[bias_spec, local, remote_keys, remote_values],
        out_specs=[local, stats],
        out_shape=[
            jax.ShapeDtypeStruct((rows, model_width), F32),
            jax.ShapeDtypeStruct((pairs, heads, rows), F32),
        ],
        scratch_shapes=[
            pltpu.VMEM((chunk, rows), F32),
            pltpu.VMEM((heads, rows), F32),
            pltpu.VMEM((heads, rows), F32),
            pltpu.VMEM((heads, lanes, rows), F32),
        ],
        compiler_params=params,
        cost_estimate=pl.CostEstimate(
            flops=4 * flops,
            bytes_accessed=4 * length * model_width,
            transcendentals=rows * length * head_count,
        ),
    )
    pull = pl.pallas_call(
        functools.partial(pull_kernel, head_width, block, head_width ** (-0.5)),
        grid=(pairs, chunks),
        in_specs=[bias_spec, local, local, local, stats, remote_keys, remote_values],
        out_specs=[
            local,
            remote_keys,
            remote_keys,
            pl.BlockSpec((1, heads, chunk // block, rows), lambda p, c: (p, 0, c, 0)),
        ],
        out_shape=[
            jax.ShapeDtypeStruct((rows, model_width), LOW),
            jax.ShapeDtypeStruct((length, model_width), LOW),
            jax.ShapeDtypeStruct((length, model_width), LOW),
            jax.ShapeDtypeStruct((pairs, heads, table_blocks, rows), F32),
        ],
        scratch_shapes=[pltpu.VMEM((heads, lanes, rows), F32)],
        compiler_params=params,
        cost_estimate=pl.CostEstimate(
            flops=10 * flops,
            bytes_accessed=8 * length * model_width,
            transcendentals=rows * length * head_count,
        ),
    )
    return attend, pull


def to_experts(rows, expert_count, capacity):
    return lax.all_to_all(
        rows.reshape(expert_count, capacity, rows.shape[-1]),
        "exp",
        split_axis=0,
        concat_axis=0,
        tiled=True,
    ).reshape(-1, rows.shape[-1])


def per_device(
    inputs,
    norm_attn,
    query_weight,
    key_weight,
    value_weight,
    output_weight,
    rel_bias,
    rel_buckets,
    norm_ffn,
    router,
    expert_input_weight,
    expert_output_weight,
    expert_ids,
    cotangent,
):
    rows = inputs.shape[1]
    width = inputs.shape[2]
    head_count = rel_bias.shape[0]
    head_width = width // head_count
    offset_count = rel_buckets.shape[0]
    expert_count = router.shape[1]
    shards = lax.axis_size("exp")
    cycle_size = lax.axis_size("ctx")
    cycle_index = lax.axis_index("ctx")
    length = rows * cycle_size
    capacity = rows * 5 // (4 * shards)
    score_scale = head_width ** (-0.5)
    ring = Ring()
    attend, pull = attention_calls(rows, length, width, head_count, head_width)

    input_rows = inputs[0].astype(F32)
    first_normed = norm_rows(input_rows, norm_attn).astype(LOW)
    all_normed = ring.gather(first_normed)
    own_weights = jnp.concatenate([key_weight, value_weight, query_weight, output_weight], 1)
    full_weights = exp_gather(own_weights).reshape(width, 4 * width)
    key_value_weight = full_weights[:, : 2 * width]
    full_query = full_weights[:, 2 * width : 3 * width]
    full_output = full_weights[:, 3 * width :]

    normed_all = all_normed.reshape(length, width)
    key_value = dot_f32(normed_all, key_value_weight, 1, 0).astype(LOW)
    query_low = dot_f32(first_normed, full_query, 1, 0).astype(LOW)
    query_scaled = (query_low.astype(F32) * score_scale).astype(LOW)

    picker = one_hot(rel_buckets, rel_bias.shape[1])
    offset_bias = jnp.dot(rel_bias, picker.T, precision=PRECISE)
    offset_hot = one_hot(
        jnp.arange(cycle_size, dtype=jnp.int32) - cycle_index + cycle_size - 1, offset_count
    )
    block_bias = jnp.dot(offset_bias, offset_hot.T, precision=PRECISE)

    attended, log_total = attend(block_bias, query_scaled, key_value, key_value)
    attended_low = attended.astype(LOW)
    first_residual = input_rows + dot_f32(attended_low, full_output, 1, 0)
    second_normed = norm_rows(first_residual, norm_ffn).astype(LOW)
    router_logits = jnp.dot(second_normed, router, preferred_element_type=F32)
    probs = jax.nn.softmax(router_logits, -1)
    expert_rows = expert_ids[0, :, 0]
    chosen = one_hot(expert_rows, expert_count)
    gate = jnp.sum(probs * chosen, -1)
    slot_rank = jnp.sum((jnp.cumsum(chosen, 0) - 1.0) * chosen, -1).astype(jnp.int32)
    targets = expert_rows * capacity + slot_rank
    dispatch = one_hot(targets, expert_count * capacity).astype(LOW)
    grad_result = cotangent[0].astype(F32)
    grad_made = (gate[:, None] * grad_result).astype(LOW)

    outgoing = jnp.concatenate([second_normed, grad_made], 1)
    send_rows = dot_f32(dispatch, outgoing, 0, 0).astype(LOW)
    arrived = to_experts(send_rows, expert_count, capacity)
    expert_rows_in = arrived[:, :width]
    grad_rows = arrived[:, width:]
    weight_in = expert_input_weight[0]
    weight_out = expert_output_weight[0]
    hidden_preactivation = dot_f32(expert_rows_in, weight_in, 1, 1)
    hidden, gelu_pull = jax.vjp(gelu_exact, hidden_preactivation)
    hidden_low = hidden.astype(LOW)
    grad_hidden = dot_f32(grad_rows, weight_out, 1, 1)
    grad_pre = gelu_pull(grad_hidden)[0].astype(LOW)
    made_low = dot_f32(hidden_low, weight_out, 1, 0).astype(LOW)
    grad_sent = dot_f32(grad_pre, weight_in, 1, 0).astype(LOW)
    returned = to_experts(jnp.concatenate([made_low, grad_sent], 1), expert_count, capacity)
    back = dot_f32(dispatch, returned, 1, 0)
    picked = back[:, :width]
    grad_from_expert = back[:, width:]

    unit_rows = weight_in.shape[0] // cycle_size
    in_weight_part = dot_f32(grad_pre, expert_rows_in, 0, 0).astype(LOW)
    out_weight_part = dot_f32(hidden_low, grad_rows, 0, 0).astype(LOW)
    expert_pieces = [
        in_weight_part.reshape(cycle_size, unit_rows, width),
        out_weight_part.reshape(cycle_size, unit_rows, width),
    ]
    expert_in_grad, expert_out_grad = (
        lax.psum_scatter(piece, "ctx", scatter_dimension=0).astype(F32) for piece in expert_pieces
    )

    result = (first_residual + gate[:, None] * picked).astype(LOW)
    grad_gate = jnp.sum(grad_result * picked, -1)
    grad_probs = chosen * grad_gate[:, None]
    grad_logits = probs * (grad_probs - jnp.sum(probs * grad_probs, -1, keepdims=True))
    router_part = jnp.dot(second_normed.astype(F32).T, grad_logits, precision=PRECISE)
    grad_two = grad_from_expert + jnp.dot(grad_logits, router.astype(F32).T, precision=PRECISE)
    norm_pull_two = jax.vjp(norm_rows, first_residual, norm_ffn)[1]
    grad_resid_part, ffn_gain_part = norm_pull_two(grad_two)
    grad_residual = grad_result + grad_resid_part
    grad_branch = grad_residual.astype(LOW)
    output_part = dot_f32(attended_low, grad_branch, 0, 0).astype(LOW)
    grad_attended = dot_f32(grad_branch, full_output, 1, 1).astype(LOW)

    grad_query_low, grad_key_part, grad_value_part, table_rows = pull(
        block_bias, query_scaled, grad_attended, attended, log_total, key_value, key_value
    )
    grad_normed_part = (
        dot_f32(grad_key_part, key_value_weight[:, :width], 1, 1)
        + dot_f32(grad_value_part, key_value_weight[:, width:], 1, 1)
    ).astype(LOW)
    normed_blocks = grad_normed_part.reshape(cycle_size, rows, width)
    half = rows // 2
    normed_sums = ring.scatter([normed_blocks[:, :half], normed_blocks[:, half:]])
    query_part = dot_f32(first_normed, grad_query_low, 0, 0).astype(LOW)
    key_part = dot_f32(normed_all, grad_key_part, 0, 0).astype(LOW)
    value_part = dot_f32(normed_all, grad_value_part, 0, 0).astype(LOW)
    dense_parts = jnp.concatenate([query_part, key_part, value_part, output_part], 1)
    dense_shard = exp_scatter(dense_parts.reshape(shards, width // shards, 4 * width))

    grad_normed = jnp.concatenate(normed_sums, 0) + dot_f32(grad_query_low, full_query, 1, 1)
    norm_pull_one = jax.vjp(norm_rows, input_rows, norm_attn)[1]
    grad_input_part, attn_gain_part = norm_pull_one(grad_normed)
    grad_inputs = grad_residual + grad_input_part

    dense_total = reduce_dense(ring, dense_shard)
    query_total, key_total, value_total, output_total = jnp.split(dense_total, 4, 1)

    grad_table = jnp.sum(table_rows.reshape(head_count, cycle_size, rows), -1)
    bias_part = jnp.dot(jnp.dot(grad_table, offset_hot, precision=PRECISE), picker, precision=PRECISE)
    small = [attn_gain_part, ffn_gain_part, router_part, bias_part]
    flat = jnp.concatenate([part.reshape(-1) for part in small])
    flat = jnp.pad(flat, (0, -flat.size % 1024))
    flat = butterfly_sum(flat.reshape(-1, 128))
    flat = flat.reshape(-1)
    totals, start = [], 0
    for part in small:
        totals.append(flat[start : start + part.size].reshape(part.shape))
        start += part.size
    attn_gain_total, ffn_gain_total, router_total, bias_total = totals
    return (
        result[None],
        grad_inputs[None],
        attn_gain_total,
        query_total,
        key_total,
        value_total,
        output_total,
        bias_total,
        ffn_gain_total,
        router_total,
        expert_in_grad[None],
        expert_out_grad[None],
    )


def reduce_dense(ring, shard):
    size = ring.size
    flat = shard.reshape(size, -1, 128)
    half = flat.shape[1] // 2
    sums = ring.scatter([flat[:, :half], flat[:, half:]])
    mine = jnp.concatenate(sums, 0).astype(LOW)
    return ring.gather(mine).reshape(shard.shape).astype(F32)


def solution(mesh):
    return jax.shard_map(
        per_device,
        mesh=mesh,
        in_specs=(
            P("exp", "ctx", None),
            P(),
            P("exp", None),
            P("exp", None),
            P("exp", None),
            P("exp", None),
            P(),
            P(),
            P(),
            P(),
            P("exp", None, None),
            P("exp", None, None),
            P("exp", "ctx", None),
            P("exp", "ctx", None),
        ),
        out_specs=(
            P("exp", "ctx", None),
            P("exp", "ctx", None),
            P(),
            P("exp", None),
            P("exp", None),
            P("exp", None),
            P("exp", None),
            P(),
            P(),
            P(),
            P("exp", "ctx", None),
            P("exp", "ctx", None),
        ),
        check_vma=False,
    )
```
